32 devices in a mesh: row: 16 (over z, y, core), col: 2 (over x).
Axes of the slice: x: 2, y: 2, z: 4, core: 2. Of those that a mesh axis runs over, the one named last changes fastest.
Arguments:
- activations: bfloat16 [512, 64, 256], P('row', 'col'), may hold values from -6 to 6
- cotangent: bfloat16 [512, 64, 256], P('row', 'col'), may hold values from -6 to 6
- kernel_wide: float32 [51, 256], replicated, may hold values from -0.875 to 0.875
- kernel_tall: float32 [51, 256], replicated, may hold values from -0.875 to 0.875
- norm_gain: float32 [256], replicated, may hold values from 0.5 to 1.5
- norm_bias: float32 [256], replicated, may hold values from -3 to 3
- weight_in: bfloat16 [256, 1024], replicated, may hold values from -0.375 to 0.375
- bias_in: float32 [1024], replicated, may hold values from -3 to 3
- weight_out: bfloat16 [1024, 256], replicated, may hold values from -0.1875 to 0.1875
- layer_scale: float32 [256], replicated, may hold values from 0.5 to 2
Outputs:
- grad_input: bfloat16 [512, 64, 256], P('row', 'col')
- grad_weight_in: bfloat16 [256, 1024], replicated
- grad_weight_out: bfloat16 [1024, 256], replicated
- grad_kernel_wide: float32 [51, 256], replicated
- grad_kernel_tall: float32 [51, 256], replicated
The draws below stay inside these ranges and needn't reach their ends.
All inputs are finite; a program needn't handle non-finite values.
Results may differ from the reference program's by a relative error of at most 0.0083.
Values may be sent and summed in bfloat16 or wider, within the bound.
A program may use at most 64 MiB of HBM per device.

```python
import math
import jax
import jax.numpy as jnp
from jax import lax

C = 256
F = 1024
KSIZE = 51
TILE_R = 32
H = 512
W = 64
N_ROW = 16


def block_levels(own_key, extent, shards, least, largest):
    def one(axis_at, shards_of):
        steps = jax.random.uniform(jax.random.fold_in(jax.random.fold_in(own_key, 6), axis_at), (shards_of,), jnp.float32, least / len(shards), largest / len(shards))
        return jnp.repeat(jnp.exp(steps), extent[axis_at] // shards_of).reshape((-1,) + (1,) * (len(extent) - axis_at - 1))

    factor_of = one(*shards[0])
    for cut in shards[1:]:
        factor_of = factor_of * one(*cut)
    return factor_of


def normal_values(stream_key, dims, deviation, most, pieces=(), dtype=jnp.bfloat16):
    values = jax.random.normal(stream_key, dims, jnp.float32) * deviation
    if len(pieces) > 0:
        values = block_levels(stream_key, dims, pieces, -0.22, 0.18) * values
    return jnp.clip(values, min=-most, max=most).astype(dtype)


def setup_inputs(seed: int = 0) -> dict:
    arg_keys = jax.random.split(jax.random.key(seed), 11)
    activations = normal_values(arg_keys[0], (H, W, C), 1.0, 6.0, ((0, 16), (1, 2)))
    cotangent = normal_values(arg_keys[1], (H, W, C), 1.0, 6.0, ((0, 16), (1, 2)))
    kernel_wide = normal_values(arg_keys[2], (KSIZE, C), KSIZE ** -0.5, 0.875, (), jnp.float32)
    kernel_tall = normal_values(arg_keys[3], (KSIZE, C), KSIZE ** -0.5, 0.875, (), jnp.float32)
    norm_gain = jnp.clip(jax.random.uniform(arg_keys[4], (C,), jnp.float32, 0.5, 1.5), 0.5, 1.5)
    norm_bias = normal_values(arg_keys[5], (C,), 0.5, 3.0, (), jnp.float32)
    weight_in = normal_values(arg_keys[6], (C, F), C ** -0.5, 0.375)
    bias_in = normal_values(arg_keys[7], (F,), 0.5, 3.0, (), jnp.float32)
    weight_out = normal_values(arg_keys[8], (F, C), F ** -0.5, 0.1875)
    layer_scale = jnp.clip(jax.random.uniform(arg_keys[9], (C,), jnp.float32, 0.5, 2.0), 0.5, 2.0)
    return dict(activations=activations, cotangent=cotangent, kernel_wide=kernel_wide, kernel_tall=kernel_tall, norm_gain=norm_gain, norm_bias=norm_bias, weight_in=weight_in, bias_in=bias_in, weight_out=weight_out, layer_scale=layer_scale)


def slide_columns(padded, kernel, length):
    total = jnp.zeros((padded.shape[0], length, padded.shape[2]), jnp.float32)
    for offset in range(kernel.shape[0]):
        total = total + kernel[offset] * padded[:, offset:offset + length, :].astype(jnp.float32)
    return total

def slide_rows(padded, kernel, length):
    total = jnp.zeros((length, padded.shape[1], padded.shape[2]), jnp.float32)
    for offset in range(kernel.shape[0]):
        total = total + kernel[offset] * padded[offset:offset + length].astype(jnp.float32)
    return total

def flip_columns(padded, kernel, length):
    last = kernel.shape[0] - 1
    total = jnp.zeros((padded.shape[0], length, padded.shape[2]), jnp.float32)
    for offset in range(kernel.shape[0]):
        total = total + kernel[offset] * padded[:, last - offset:last - offset + length, :].astype(jnp.float32)
    return total

def flip_rows(padded, kernel, length):
    last = kernel.shape[0] - 1
    total = jnp.zeros((length, padded.shape[1], padded.shape[2]), jnp.float32)
    for offset in range(kernel.shape[0]):
        total = total + kernel[offset] * padded[last - offset:last - offset + length].astype(jnp.float32)
    return total

def correlate_columns(grad, padded, taps):
    length = grad.shape[1]
    gradf = grad.astype(jnp.float32)
    return jnp.stack([lax.optimization_barrier(jnp.sum(gradf * padded[:, offset:offset + length, :].astype(jnp.float32), axis=(0, 1))) for offset in range(taps)])

def correlate_rows(grad, padded, taps):
    length = grad.shape[0]
    gradf = grad.astype(jnp.float32)
    return jnp.stack([lax.optimization_barrier(jnp.sum(gradf * padded[offset:offset + length].astype(jnp.float32), axis=(0, 1))) for offset in range(taps)])

def gelu_tanh(value):
    return jax.nn.gelu(value, approximate=True)

def mlp_backward(mixed, cot, norm_gain, norm_bias, weight_in, bias_in, weight_out, layer_scale):
    average = lax.optimization_barrier(jnp.mean(mixed, axis=-1, keepdims=True))
    centred = mixed - average
    spread = lax.optimization_barrier(jnp.mean(centred * centred, axis=-1, keepdims=True))
    rstd_val = lax.rsqrt(spread + 1e-06)
    unit = centred * rstd_val
    normed = (unit * norm_gain + norm_bias).astype(jnp.bfloat16)
    pre = jnp.dot(normed, weight_in, preferred_element_type=jnp.float32) + bias_in
    lifted_f, pullback = jax.vjp(gelu_tanh, pre)
    lifted = lifted_f.astype(jnp.bfloat16)
    scaled_cot = (layer_scale * cot.astype(jnp.float32)).astype(jnp.bfloat16)
    sum_out = jnp.dot(lifted.T, scaled_cot, preferred_element_type=jnp.float32)
    grad_lift = jnp.dot(scaled_cot, weight_out.T, preferred_element_type=jnp.float32)
    grad_pre = pullback(grad_lift)[0].astype(jnp.bfloat16)
    sum_in = jnp.dot(normed.T, grad_pre, preferred_element_type=jnp.float32)
    grad_unit = jnp.dot(grad_pre, weight_in.T, preferred_element_type=jnp.float32) * norm_gain
    first = lax.optimization_barrier(jnp.mean(grad_unit, axis=-1, keepdims=True))
    second = lax.optimization_barrier(jnp.mean(grad_unit * unit, axis=-1, keepdims=True))
    grad_mixed = (rstd_val * (grad_unit - first - unit * second)).astype(jnp.bfloat16)
    return (grad_mixed, sum_in, sum_out)

def reference(activations, cotangent, kernel_wide, kernel_tall, norm_gain, norm_bias, weight_in, bias_in, weight_out, layer_scale):
    reach = KSIZE // 2
    wide_input = jnp.pad(activations, ((0, 0), (reach, reach), (0, 0)))
    hidden = slide_columns(wide_input, kernel_wide, W).astype(jnp.bfloat16)
    tall_hidden = jnp.pad(hidden, ((reach, reach), (0, 0), (0, 0)))
    mixed = slide_rows(tall_hidden, kernel_tall, H)
    mixed_blocks = mixed.reshape(N_ROW, TILE_R * W, C)
    cot_blocks = cotangent.reshape(N_ROW, TILE_R * W, C)

    def visit(carry, pair):
        grad_mixed, sum_in, sum_out = mlp_backward(pair[0], pair[1], norm_gain, norm_bias, weight_in, bias_in, weight_out, layer_scale)
        return ((carry[0] + sum_in, carry[1] + sum_out), grad_mixed)
    start = (jnp.zeros((C, F), jnp.float32), jnp.zeros((F, C), jnp.float32))
    (total_in, total_out), grad_blocks = lax.scan(visit, start, (mixed_blocks, cot_blocks))
    grad_mixed = grad_blocks.reshape(H, W, C)
    tall_grad = jnp.pad(grad_mixed, ((reach, reach), (0, 0), (0, 0)))
    grad_hidden = flip_rows(tall_grad, kernel_tall, H).astype(jnp.bfloat16)
    wide_grad = jnp.pad(grad_hidden, ((0, 0), (reach, reach), (0, 0)))
    grad_input = (cotangent.astype(jnp.float32) + flip_columns(wide_grad, kernel_wide, W)).astype(jnp.bfloat16)
    factor = 1.0 / math.sqrt(H * W)
    grad_kernel_tall = correlate_rows(grad_mixed, tall_hidden, KSIZE) * factor
    grad_kernel_wide = correlate_columns(grad_hidden, wide_input, KSIZE) * factor
    return (grad_input, (total_in * factor).astype(jnp.bfloat16), (total_out * factor).astype(jnp.bfloat16), grad_kernel_wide, grad_kernel_tall)
```

```python
import functools
import math

import jax
import jax.numpy as jnp
from jax import lax
from jax.experimental import pallas as pl
from jax.experimental.pallas import tpu as pltpu
from jax.sharding import PartitionSpec as P


def with_halo(block, sides, width):
    for axis, dim in sides:
        count = lax.axis_size(axis)
        forward = [(i, i + 1) for i in range(count - 1)]
        backward = [(target, source) for source, target in forward]
        low = lax.ppermute(
            lax.slice_in_dim(block, block.shape[dim] - width, None, axis=dim), axis, forward
        )
        high = lax.ppermute(lax.slice_in_dim(block, 0, width, axis=dim), axis, backward)
        block = jnp.concatenate([low, block, high], axis=dim)
    return block


def slide_columns(padded, kernel, length):
    total = jnp.zeros((padded.shape[0], length, padded.shape[2]), jnp.float32)
    for offset in range(kernel.shape[0]):
        total = total + kernel[offset] * padded[:, offset : offset + length, :].astype(jnp.float32)
    return total


def slide_rows(padded, kernel, length):
    total = jnp.zeros((length, padded.shape[1], padded.shape[2]), jnp.float32)
    for offset in range(kernel.shape[0]):
        total = total + kernel[offset] * padded[offset : offset + length].astype(jnp.float32)
    return total


def flip_columns(padded, kernel, length):
    last = kernel.shape[0] - 1
    total = jnp.zeros((padded.shape[0], length, padded.shape[2]), jnp.float32)
    for offset in range(kernel.shape[0]):
        total = total + kernel[offset] * padded[
            :, last - offset : last - offset + length, :
        ].astype(jnp.float32)
    return total


def flip_rows(padded, kernel, length):
    last = kernel.shape[0] - 1
    total = jnp.zeros((length, padded.shape[1], padded.shape[2]), jnp.float32)
    for offset in range(kernel.shape[0]):
        total = total + kernel[offset] * padded[last - offset : last - offset + length].astype(
            jnp.float32
        )
    return total


def correlate_columns(grad, padded, taps):
    length = grad.shape[1]
    gradf = grad.astype(jnp.float32)
    return jnp.stack(
        [
            jnp.sum(gradf * padded[:, offset : offset + length, :].astype(jnp.float32), axis=(0, 1))
            for offset in range(taps)
        ]
    )


def correlate_rows(grad, padded, taps):
    length = grad.shape[0]
    gradf = grad.astype(jnp.float32)
    return jnp.stack(
        [
            jnp.sum(gradf * padded[offset : offset + length].astype(jnp.float32), axis=(0, 1))
            for offset in range(taps)
        ]
    )


def gelu_tanh(value):
    return jax.nn.gelu(value, approximate=True)


def mlp_backward(mixed, cot, norm_gain, norm_bias, weight_in, bias_in, weight_out, layer_scale):
    average = jnp.mean(mixed, axis=-1, keepdims=True)
    centred = mixed - average
    spread = jnp.mean(centred * centred, axis=-1, keepdims=True)
    rstd_val = lax.rsqrt(spread + 1e-06)
    unit = centred * rstd_val
    normed = (unit * norm_gain + norm_bias).astype(jnp.bfloat16)
    pre = jnp.dot(normed, weight_in, preferred_element_type=jnp.float32) + bias_in
    lifted_f, pullback = jax.vjp(gelu_tanh, pre)
    lifted = lifted_f.astype(jnp.bfloat16)
    scaled_cot = (layer_scale * cot.astype(jnp.float32)).astype(jnp.bfloat16)
    sum_out = jnp.dot(lifted.T, scaled_cot, preferred_element_type=jnp.float32)
    grad_lift = jnp.dot(scaled_cot, weight_out.T, preferred_element_type=jnp.float32)
    grad_pre = pullback(grad_lift)[0].astype(jnp.bfloat16)
    sum_in = jnp.dot(normed.T, grad_pre, preferred_element_type=jnp.float32)
    grad_unit = jnp.dot(grad_pre, weight_in.T, preferred_element_type=jnp.float32) * norm_gain
    first = jnp.mean(grad_unit, axis=-1, keepdims=True)
    second = jnp.mean(grad_unit * unit, axis=-1, keepdims=True)
    grad_mixed = (rstd_val * (grad_unit - first - unit * second)).astype(jnp.bfloat16)
    return (grad_mixed, sum_in, sum_out)


MESH = pl.DeviceIdType.MESH


def reduce_kernel(n_row, n_col, factor, big, small, in_out, out_out, small_out, *scratch):
    nets = []
    for k, src in enumerate((big, small)):
        pair_buf, half, slots, cols, whole, s0, r0, s1, r1, s2, r2, s3, r3, s4, r4 = scratch[
            15 * k : 15 * k + 15
        ]
        nets.append((src, pair_buf, half, slots, cols, whole, s0, r0, s1, r1, s2, r2, s3, r3, s4, r4))
    row, col = lax.axis_index("row"), lax.axis_index("col")
    m = n_row // 2
    core, j = lax.rem(row, 2), row // 2
    pair = (row + 1 - 2 * core, col)

    def peer(d):
        return (2 * lax.rem(j + d, m) + core, col)

    def col_peer(d):
        return (row, lax.rem(col + d, n_col))

    def copy(src, dst, send, recv, target):
        return pltpu.make_async_remote_copy(
            src_ref=src, dst_ref=dst, send_sem=send, recv_sem=recv, device_id=target, device_id_type=MESH
        )

    barrier = pltpu.get_barrier_semaphore()
    pl.semaphore_signal(barrier, inc=1, device_id=pair, device_id_type=MESH)

    @pl.loop(1, m)
    def _(d):
        pl.semaphore_signal(barrier, inc=1, device_id=peer(d), device_id_type=MESH)

    @pl.loop(1, n_col)
    def _(d):
        pl.semaphore_signal(barrier, inc=1, device_id=col_peer(d), device_id_type=MESH)

    pl.semaphore_wait(barrier, 1 + (m - 1) + (n_col - 1))

    def pair_copy(net):
        src, pair_buf, s0, r0 = net[0], net[1], net[6], net[7]
        h = pair_buf.shape[0]
        other = pl.multiple_of((1 - core) * h, 16)
        return copy(src.at[pl.ds(other, h)], pair_buf, s0, r0, pair)

    def peer_copy(net, d):
        half, slots, s1, r1 = net[2], net[3], net[8], net[9]
        p = slots.shape[1]
        at = pl.multiple_of(lax.rem(j + d, m) * p, p)
        return copy(half.at[pl.ds(at, p)], slots.at[d], s1.at[d], r1.at[d], peer(d))

    def col_copy(net, d, c):
        cols, s2, r2 = net[4], net[10], net[11]
        return copy(cols.at[c], cols.at[c], s2.at[d], r2.at[c], col_peer(d))

    def back_copy(net, d, owner):
        slots, whole, s3, r3 = net[3], net[5], net[12], net[13]
        p = slots.shape[1]
        at = pl.multiple_of(core * (whole.shape[0] // 2) + owner * p, p)
        return copy(whole.at[pl.ds(at, p)], whole.at[pl.ds(at, p)], s3.at[d], r3.at[d], peer(d))

    def last_copy(net, side):
        whole, s4, r4 = net[5], net[14], net[15]
        h = whole.shape[0] // 2
        at = pl.multiple_of(side * h, 16)
        return copy(whole.at[pl.ds(at, h)], whole.at[pl.ds(at, h)], s4, r4, pair)

    for net in nets:
        pair_copy(net).start()
    for net in nets:
        src, pair_buf, half = net[0], net[1], net[2]
        pair_copy(net).wait()
        h = half.shape[0]
        at = pl.multiple_of(core * h, 16)
        mine = src[pl.ds(at, h), :].astype(jnp.float32)
        half[...] = (mine + pair_buf[...].astype(jnp.float32)).astype(half.dtype)

        @pl.loop(1, m)
        def _(d, net=net):
            peer_copy(net, d).start()

    for net in nets:
        half, slots, cols = net[2], net[3], net[4]
        p = slots.shape[1]
        cols[col] = half[pl.ds(pl.multiple_of(j * p, p), p), :].astype(jnp.float32)

        @pl.loop(1, m)
        def _(d, net=net, slots=slots, cols=cols):
            peer_copy(net, d).wait()
            cols[col] = cols[col] + slots[d].astype(jnp.float32)

        @pl.loop(1, n_col)
        def _(d, net=net):
            col_copy(net, d, col).start()

    for net in nets:
        slots, cols, whole = net[3], net[4], net[5]
        p = slots.shape[1]

        @pl.loop(1, n_col)
        def _(d, net=net):
            col_copy(net, d, col).wait_send()
            col_copy(net, d, lax.rem(col + d, n_col)).wait_recv()

        total = cols[0]
        for c in range(1, n_col):
            total = total + cols[c]
        at = pl.multiple_of(core * (whole.shape[0] // 2) + j * p, p)
        whole[pl.ds(at, p), :] = (total * factor).astype(whole.dtype)

        @pl.loop(1, m)
        def _(d, net=net):
            back_copy(net, d, j).start()

    for net in nets:

        @pl.loop(1, m)
        def _(d, net=net):
            back_copy(net, d, j).wait_send()
            back_copy(net, d, lax.rem(j + m - d, m)).wait_recv()

        last_copy(net, core).start()
    for net in nets:
        last_copy(net, core).wait_send()
        last_copy(net, 1 - core).wait_recv()
    whole_big, whole_small = nets[0][5], nets[1][5]
    depth, wide = in_out.shape
    blocks = wide // whole_big.shape[1]
    width = whole_big.shape[1]
    for b in range(blocks):
        in_out[:, b * width : (b + 1) * width] = whole_big[b * depth : (b + 1) * depth, :]
    out_out[...] = whole_big[blocks * depth :, :]
    small_out[...] = whole_small[...]


def reduce_sums(sum_in, sum_out, part_wide, part_tall, factor):
    n_row, n_col = lax.axis_size("row"), lax.axis_size("col")
    m = n_row // 2
    depth, wide = sum_in.shape
    taps, width = part_wide.shape
    big = jnp.concatenate(
        [sum_in[:, b * width : (b + 1) * width] for b in range(wide // width)] + [sum_out], axis=0
    ).astype(jnp.bfloat16)
    each = -(-2 * taps // (8 * n_row)) * 8
    small = jnp.concatenate(
        [part_wide, part_tall, jnp.zeros((each * n_row - 2 * taps, width), jnp.float32)], axis=0
    )
    scratch = []
    for src in (big, small):
        rows = src.shape[0]
        p = rows // n_row
        dma = pltpu.SemaphoreType.DMA
        scratch += [
            pltpu.VMEM((rows // 2, width), src.dtype),
            pltpu.VMEM((rows // 2, width), src.dtype),
            pltpu.VMEM((m, p, width), src.dtype),
            pltpu.VMEM((n_col, p, width), jnp.float32),
            pltpu.VMEM((rows, width), src.dtype),
            dma,
            dma,
            dma((m,)),
            dma((m,)),
            dma((n_col,)),
            dma((n_col,)),
            dma((m,)),
            dma((m,)),
            dma,
            dma,
        ]
    vmem = pl.BlockSpec(memory_space=pltpu.VMEM)
    grad_in, grad_out, tapped = pl.pallas_call(
        functools.partial(reduce_kernel, n_row, n_col, factor),
        out_shape=(
            jax.ShapeDtypeStruct(sum_in.shape, jnp.bfloat16),
            jax.ShapeDtypeStruct(sum_out.shape, jnp.bfloat16),
            jax.ShapeDtypeStruct(small.shape, jnp.float32),
        ),
        in_specs=[vmem] * 2,
        out_specs=(vmem,) * 3,
        scratch_shapes=scratch,
        compiler_params=pltpu.CompilerParams(
            collective_id=0, has_side_effects=True, vmem_limit_bytes=32 * 1024 * 1024
        ),
    )(big, small)
    return grad_in, grad_out, tapped[:taps], tapped[taps : 2 * taps]


def local(
    activations,
    cotangent,
    kernel_wide,
    kernel_tall,
    norm_gain,
    norm_bias,
    weight_in,
    bias_in,
    weight_out,
    layer_scale,
):
    tile_rows, tile_cols, chans = activations.shape
    taps = kernel_wide.shape[0]
    reach = taps // 2
    wide_input = with_halo(activations, (("col", 1),), reach)
    hidden = slide_columns(wide_input, kernel_wide, tile_cols).astype(jnp.bfloat16)
    tall_hidden = with_halo(hidden, (("row", 0),), reach)
    mixed = slide_rows(tall_hidden, kernel_tall, tile_rows)
    grad_flat, sum_in, sum_out = mlp_backward(
        mixed.reshape(-1, chans),
        cotangent.reshape(-1, chans),
        norm_gain,
        norm_bias,
        weight_in,
        bias_in,
        weight_out,
        layer_scale,
    )
    grad_mixed = grad_flat.reshape(tile_rows, tile_cols, chans)
    tall_grad = with_halo(grad_mixed, (("row", 0),), reach)
    grad_hidden = flip_rows(tall_grad, kernel_tall, tile_rows).astype(jnp.bfloat16)
    wide_grad = with_halo(grad_hidden, (("col", 1),), reach)
    grad_input = (
        cotangent.astype(jnp.float32) + flip_columns(wide_grad, kernel_wide, tile_cols)
    ).astype(jnp.bfloat16)
    part_tall = correlate_rows(grad_mixed, tall_hidden, taps)
    part_wide = correlate_columns(grad_hidden, wide_input, taps)
    pixels = tile_rows * lax.axis_size("row") * tile_cols * lax.axis_size("col")
    factor = 1.0 / math.sqrt(pixels)
    grad_in, grad_out, grad_wide, grad_tall = reduce_sums(
        sum_in, sum_out, part_wide, part_tall, factor
    )
    return (grad_input, grad_in, grad_out, grad_wide, grad_tall)


def solution(mesh):
    in_specs = (
        P("row", "col", None),
        P("row", "col", None),
        P(),
        P(),
        P(),
        P(),
        P(),
        P(),
        P(),
        P(),
    )
    out_specs = (P("row", "col", None), P(), P(), P(), P())
    return jax.shard_map(local, mesh=mesh, in_specs=in_specs, out_specs=out_specs, check_vma=False)
```

```python
import functools
import math

import jax
import jax.numpy as jnp
from jax import lax
from jax.experimental import pallas as pl
from jax.experimental.pallas import tpu as pltpu
from jax.sharding import PartitionSpec as P


def gelu_tanh(value):
    return jax.nn.gelu(value, approximate=True)


def mlp_backward(mixed, cot, norm_gain, norm_bias, weight_in, bias_in, weight_out, layer_scale):
    average = jnp.mean(mixed, axis=-1, keepdims=True)
    centred = mixed - average
    spread = jnp.mean(centred * centred, axis=-1, keepdims=True)
    rstd_val = lax.rsqrt(spread + 1e-06)
    unit = centred * rstd_val
    normed = (unit * norm_gain + norm_bias).astype(jnp.bfloat16)
    pre = jnp.dot(normed, weight_in, preferred_element_type=jnp.float32) + bias_in
    lifted_f, pullback = jax.vjp(gelu_tanh, pre)
    lifted = lifted_f.astype(jnp.bfloat16)
    scaled_cot = (layer_scale * cot.astype(jnp.float32)).astype(jnp.bfloat16)
    sum_out = jnp.dot(lifted.T, scaled_cot, preferred_element_type=jnp.float32)
    grad_lift = jnp.dot(scaled_cot, weight_out.T, preferred_element_type=jnp.float32)
    grad_pre = pullback(grad_lift)[0].astype(jnp.bfloat16)
    sum_in = jnp.dot(normed.T, grad_pre, preferred_element_type=jnp.float32)
    grad_unit = jnp.dot(grad_pre, weight_in.T, preferred_element_type=jnp.float32) * norm_gain
    first = jnp.mean(grad_unit, axis=-1, keepdims=True)
    second = jnp.mean(grad_unit * unit, axis=-1, keepdims=True)
    grad_mixed = (rstd_val * (grad_unit - first - unit * second)).astype(jnp.bfloat16)
    return (grad_mixed, sum_in, sum_out)


MESH = pl.DeviceIdType.MESH
GROUP = 8
LANES = 128


def remote(src, dst, send, recv, target):
    return pltpu.make_async_remote_copy(
        src_ref=src, dst_ref=dst, send_sem=send, recv_sem=recv, device_id=target, device_id_type=MESH
    )


def below(at, count):
    return (at + count - 1) // count


def above(at, count):
    return (2 * count - 2 - at) // count


def greet(barrier, target):
    pl.semaphore_signal(barrier, inc=1, device_id=target, device_id_type=MESH)


def taps_loop(acc, lo, hi, one, unroll=5):
    steps = max(hi - lo, 0) // unroll

    def body(s, acc):
        for u in range(unroll):
            acc = one(lo + s * unroll + u, acc)
        return acc

    if steps > 0:
        acc = lax.fori_loop(0, steps, body, acc)
    for o in range(lo + steps * unroll, hi):
        acc = one(o, acc)
    return acc


def conv_pass(padded, kernel, flip, minor, ranges, blocks, start, finish):
    last = kernel.shape[0] // 8 - 1
    size = GROUP * minor
    for b in blocks:

        @pl.loop(0, padded.shape[0])
        def _(part, b=b):
            lane = pl.ds(pl.multiple_of(part * LANES, LANES), LANES)

            def one(o, acc):
                tap_at = (last - o if flip else o) * 8
                tap_at = tap_at if isinstance(tap_at, int) else pl.multiple_of(tap_at, 8)
                tap = kernel[pl.ds(tap_at, 8), lane]
                at = b * size + o * minor
                at = at if isinstance(at, int) else pl.multiple_of(at, 8)
                return acc + tap[None] * padded[part, pl.ds(at, size), :].reshape(size // 8, 8, LANES)

            acc = start(b, lane).reshape(size // 8, 8, LANES)
            for lo, hi in ranges(b):
                acc = taps_loop(acc, lo, hi, one)
            finish(b, part, lane, acc.reshape(size, LANES))


def correlate(grad_at, grad, padded, taps, minor, sums, out, out_at):
    lead = (padded.shape[1] // minor) - taps + 1
    size = GROUP * minor
    for b in range(lead // GROUP):

        @pl.loop(0, padded.shape[0])
        def _(part, b=b):
            lane = pl.ds(pl.multiple_of(part * LANES, LANES), LANES)
            own = grad[part, pl.ds(grad_at + b * size, size), :]

            def one(o, carry):
                at = b * size + o * minor
                at = at if isinstance(at, int) else pl.multiple_of(at, 8)
                prod = own * padded[part, pl.ds(at, size), :]
                folded = jnp.sum(prod.reshape(size // 8, 8, LANES), axis=0)
                row = o * 8
                row = row if isinstance(row, int) else pl.multiple_of(row, 8)
                if b == 0:
                    sums[pl.ds(row, 8), lane] = folded
                else:
                    sums[pl.ds(row, 8), lane] = sums[pl.ds(row, 8), lane] + folded
                return carry

            taps_loop(0, 0, taps, one, 3)

    for t in range(taps):
        out[out_at + t : out_at + t + 1, :] = jnp.sum(sums[8 * t : 8 * t + 8, :], axis=0, keepdims=True)


def widen(src, padded, at):
    n = src.shape[0]
    for part in range(padded.shape[0]):
        lane = slice(part * LANES, (part + 1) * LANES)
        padded[part, at : at + n, :] = src[:, lane].astype(jnp.float32)


def narrow(padded, at, dst):
    n = dst.shape[0]
    for part in range(padded.shape[0]):
        lane = slice(part * LANES, (part + 1) * LANES)
        dst[:, lane] = padded[part, at : at + n, :].astype(dst.dtype)


class Halo:
    def __init__(self, at, count, target, src, low, high, sems):
        h = low.shape[0]
        top = src.shape[0] - h
        self.at, self.count, self.low, self.high = at, count, low, high
        self.up = remote(
            src.at[pl.ds(top, h)], low, sems.at[0], sems.at[1], target(lax.rem(at + 1, count))
        )
        self.down = remote(
            src.at[pl.ds(0, h)], high, sems.at[2], sems.at[3], target(lax.rem(at + count - 1, count))
        )

    def start(self):
        pl.when(self.at < self.count - 1)(self.up.start)
        pl.when(self.at > 0)(self.down.start)

    def clear(self, padded):
        h = self.low.shape[0]
        rest = padded.shape[1] - h
        zeros = jnp.zeros((padded.shape[0], h, LANES), jnp.float32)
        padded[:, 0:h, :] = zeros
        padded[:, rest : rest + h, :] = zeros

    def finish(self, padded):
        h = self.low.shape[0]
        rest = padded.shape[1] - h

        @pl.when(self.at > 0)
        def _():
            self.up.wait_recv()
            widen(self.low, padded, 0)
            self.down.wait_send()

        @pl.when(self.at < self.count - 1)
        def _():
            self.down.wait_recv()
            widen(self.high, padded, rest)
            self.up.wait_send()


def inner_range(lead, reach):
    return lambda b: [(max(reach - GROUP * b, 0), lead + reach - GROUP * b - GROUP + 1)]


def outer_range(lead, reach):
    def ranges(b):
        lo, hi = inner_range(lead, reach)(b)[0]
        return [(0, lo), (hi, 2 * reach + 1)]

    return ranges


def no_start(size):
    return lambda b, lane: jnp.zeros((size, LANES), jnp.float32)


def transposing(dst, at, inner, outer):
    def finish(b, part, lane, acc):
        value = acc.astype(jnp.bfloat16).astype(jnp.float32)
        for g in range(GROUP):
            dst[part, pl.ds(at + b * GROUP + g, inner, stride=outer), :] = value[g * inner : (g + 1) * inner]

    return finish


def into(dst, size):
    def finish(b, part, lane, acc):
        dst[pl.ds(b * size, size), lane] = acc

    return finish


def out_of(src, size):
    return lambda b, lane: src[pl.ds(b * size, size), lane]


def front_kernel(
    n_row, n_col, rows, cols, act, kw, kt, mixed, wide, tall, low_a, high_a, low_h, high_h, hid, part, sem_a, sem_h
):
    row, col = lax.axis_index("row"), lax.axis_index("col")
    barrier = pltpu.get_barrier_semaphore()
    reach = kw.shape[0] // 16
    for at, count, target in (
        (row, n_row, lambda i: (i, col)),
        (col, n_col, lambda i: (row, i)),
    ):
        pl.when(at > 0)(lambda at=at, target=target: greet(barrier, target(at - 1)))
        pl.when(at < count - 1)(lambda at=at, target=target: greet(barrier, target(at + 1)))
    greeted = below(row, n_row) + above(row, n_row) + below(col, n_col) + above(col, n_col)
    pl.semaphore_wait(barrier, greeted)
    halo = Halo(col, n_col, lambda i: (row, i), act, low_a, high_a, sem_a)
    halo.start()
    halo.clear(wide)
    widen(act, wide, reach * rows)
    blocks, size = range(cols // GROUP), GROUP * rows
    conv_pass(wide, kw, False, rows, inner_range(cols, reach), blocks, no_start(size), into(part, size))
    halo.finish(wide)
    conv_pass(
        wide, kw, False, rows, outer_range(cols, reach), blocks, out_of(part, size),
        transposing(tall, reach * cols, rows, cols),
    )
    narrow(tall, reach * cols, hid)
    halo = Halo(row, n_row, lambda i: (i, col), hid, low_h, high_h, sem_h)
    halo.start()
    halo.clear(tall)
    blocks, size = range(rows // GROUP), GROUP * cols
    conv_pass(tall, kt, False, cols, inner_range(rows, reach), blocks, no_start(size), into(part, size))
    halo.finish(tall)
    conv_pass(
        tall, kt, False, cols, outer_range(rows, reach), blocks, out_of(part, size), into(mixed, size)
    )


class Net:
    def __init__(self, n_row, n_col, factor, src, scratch):
        self.src, self.n_col, self.factor = src, n_col, factor
        self.pair_buf, self.half, self.slots, self.cols, self.whole = scratch[:5]
        self.sems = scratch[5:]
        self.row, self.col = lax.axis_index("row"), lax.axis_index("col")
        self.m = n_row // 2
        self.core, self.j = lax.rem(self.row, 2), self.row // 2
        self.pair = (self.row + 1 - 2 * self.core, self.col)
        self.p = self.slots.shape[1]
        self.h = self.half.shape[0]

    def peer(self, d):
        return (2 * lax.rem(self.j + d, self.m) + self.core, self.col)

    def col_peer(self, d):
        return (self.row, lax.rem(self.col + d, self.n_col))

    def pair_copy(self):
        other = pl.multiple_of((1 - self.core) * self.h, 16)
        return remote(self.src.at[pl.ds(other, self.h)], self.pair_buf, self.sems[0], self.sems[1], self.pair)

    def peer_copy(self, d):
        at = pl.multiple_of(lax.rem(self.j + d, self.m) * self.p, self.p)
        return remote(
            self.half.at[pl.ds(at, self.p)], self.slots.at[d], self.sems[2].at[d], self.sems[3].at[d], self.peer(d)
        )

    def col_copy(self, d, c):
        return remote(self.cols.at[c], self.cols.at[c], self.sems[4].at[d], self.sems[5].at[c], self.col_peer(d))

    def back_copy(self, d, owner):
        at = pl.multiple_of(self.core * self.h + owner * self.p, self.p)
        part = self.whole.at[pl.ds(at, self.p)]
        return remote(part, part, self.sems[6].at[d], self.sems[7].at[d], self.peer(d))

    def last_copy(self, side):
        part = self.whole.at[pl.ds(pl.multiple_of(side * self.h, 16), self.h)]
        return remote(part, part, self.sems[8], self.sems[9], self.pair)

    def step_pair(self):
        self.pair_copy().start()

    def step_peers(self):
        self.pair_copy().wait()
        at = pl.multiple_of(self.core * self.h, 16)
        mine = self.src[pl.ds(at, self.h), :].astype(jnp.float32)
        self.half[...] = (mine + self.pair_buf[...].astype(jnp.float32)).astype(self.half.dtype)

        @pl.loop(1, self.m)
        def _(d):
            self.peer_copy(d).start()

    def step_cols(self):
        at = pl.multiple_of(self.j * self.p, self.p)
        self.cols[self.col] = self.half[pl.ds(at, self.p), :].astype(jnp.float32)

        @pl.loop(1, self.m)
        def _(d):
            self.peer_copy(d).wait()
            self.cols[self.col] = self.cols[self.col] + self.slots[d].astype(jnp.float32)

        @pl.loop(1, self.n_col)
        def _(d):
            self.col_copy(d, self.col).start()

    def step_back(self):
        @pl.loop(1, self.n_col)
        def _(d):
            self.col_copy(d, self.col).wait_send()
            self.col_copy(d, lax.rem(self.col + d, self.n_col)).wait_recv()

        total = self.cols[0]
        for c in range(1, self.n_col):
            total = total + self.cols[c]
        at = pl.multiple_of(self.core * self.h + self.j * self.p, self.p)
        self.whole[pl.ds(at, self.p), :] = (total * self.factor).astype(self.whole.dtype)

        @pl.loop(1, self.m)
        def _(d):
            self.back_copy(d, self.j).start()

    def step_last(self):
        @pl.loop(1, self.m)
        def _(d):
            self.back_copy(d, self.j).wait_send()
            self.back_copy(d, lax.rem(self.j + self.m - d, self.m)).wait_recv()

        self.last_copy(self.core).start()

    def step_end(self):
        self.last_copy(self.core).wait_send()
        self.last_copy(1 - self.core).wait_recv()


def back_kernel(
    n_row, n_col, rows, cols, factor, gm, tall, wide, kw, kt, big, gin, in_out, out_out, small_out,
    gpad, hpad, low_g, high_g, low_h, high_h, ghb, part, sums, small, sem_g, sem_h, *scratch
):
    row, col = lax.axis_index("row"), lax.axis_index("col")
    reach, taps = kw.shape[0] // 16, kw.shape[0] // 8
    net = Net(n_row, n_col, factor, big, scratch[:15])
    net2 = Net(n_row, n_col, factor, small, scratch[15:])
    barrier = pltpu.get_barrier_semaphore()
    other = row - 1 + 2 * net.core
    present = jnp.logical_and(other >= 0, other < n_row)
    greet(barrier, net.pair)
    pl.when(present)(lambda: greet(barrier, (other, col)))

    @pl.loop(1, net.m)
    def _(d):
        greet(barrier, net.peer(d))

    @pl.loop(1, n_col)
    def _(d):
        greet(barrier, net.col_peer(d))

    more = (1 - net.core) * below(row, n_row) + net.core * above(row, n_row)
    pl.semaphore_wait(barrier, 1 + (net.m - 1) + (n_col - 1) + more)

    halo = Halo(row, n_row, lambda i: (i, col), gm, low_g, high_g, sem_g)
    halo.start()
    net.step_pair()
    halo.clear(gpad)
    widen(gm, gpad, reach * cols)
    small[2 * taps :, :] = jnp.zeros((small.shape[0] - 2 * taps, small.shape[1]), jnp.float32)
    correlate(reach * cols, gpad, tall, taps, cols, sums, small, taps)
    halo.finish(gpad)
    net.step_peers()
    blocks, size = range(rows // GROUP), GROUP * cols
    conv_pass(
        gpad, kt, True, cols, lambda b: [(0, taps)], blocks, no_start(size),
        transposing(hpad, reach * rows, cols, rows),
    )
    narrow(hpad, reach * rows, ghb)
    halo = Halo(col, n_col, lambda i: (row, i), ghb, low_h, high_h, sem_h)
    halo.start()
    halo.clear(hpad)
    correlate(reach * rows, hpad, wide, taps, rows, sums, small, 0)
    net2.step_pair()
    net.step_cols()
    blocks, size = range(cols // GROUP), GROUP * rows
    conv_pass(hpad, kw, True, rows, inner_range(cols, reach), blocks, no_start(size), into(part, size))
    net2.step_peers()
    halo.finish(hpad)
    net.step_back()
    half = len(blocks) // 2
    outer = outer_range(cols, reach)
    conv_pass(hpad, kw, True, rows, outer, blocks[:half], out_of(part, size), into(gin, size))
    net2.step_cols()
    conv_pass(hpad, kw, True, rows, outer, blocks[half:], out_of(part, size), into(gin, size))
    net2.step_back()
    net.step_last()
    net2.step_last()
    net.step_end()
    net2.step_end()
    depth, width = in_out.shape[0], net.whole.shape[1]
    inner = in_out.shape[1] // width
    for b in range(inner):
        in_out[:, b * width : (b + 1) * width] = net.whole[b * depth : (b + 1) * depth, :]
    out_out[...] = net.whole[inner * depth :, :]
    small_out[...] = net2.whole[...]


def net_scratch(src, n_row, n_col):
    rows, width = src.shape
    p, m = rows // n_row, n_row // 2
    dma = pltpu.SemaphoreType.DMA
    return [
        pltpu.VMEM((rows // 2, width), src.dtype),
        pltpu.VMEM((rows // 2, width), src.dtype),
        pltpu.VMEM((m, p, width), src.dtype),
        pltpu.VMEM((n_col, p, width), jnp.float32),
        pltpu.VMEM((rows, width), src.dtype),
        dma, dma, dma((m,)), dma((m,)), dma((n_col,)), dma((n_col,)), dma((m,)), dma((m,)), dma, dma,
    ]


def params(number):
    return pltpu.CompilerParams(
        collective_id=number, has_side_effects=True, vmem_limit_bytes=40 * 1024 * 1024
    )


def local(
    activations, cotangent, kernel_wide, kernel_tall, norm_gain, norm_bias, weight_in, bias_in, weight_out, layer_scale
):
    rows, cols, chans = activations.shape
    taps = kernel_wide.shape[0]
    reach = taps // 2
    n_row, n_col = lax.axis_size("row"), lax.axis_size("col")
    pixels = rows * cols
    f32, bf16 = jnp.float32, jnp.bfloat16
    vmem = pl.BlockSpec(memory_space=pltpu.VMEM)
    dma = pltpu.SemaphoreType.DMA
    wide_shape = jax.ShapeDtypeStruct((chans // LANES, (cols + 2 * reach) * rows, LANES), f32)
    tall_shape = jax.ShapeDtypeStruct((chans // LANES, (rows + 2 * reach) * cols, LANES), f32)
    halos = [
        pltpu.VMEM((reach * rows, chans), bf16),
        pltpu.VMEM((reach * rows, chans), bf16),
        pltpu.VMEM((reach * cols, chans), bf16),
        pltpu.VMEM((reach * cols, chans), bf16),
    ]
    tile = [pltpu.VMEM((pixels, chans), bf16), pltpu.VMEM((pixels, chans), f32)]
    kw, kt = jnp.repeat(kernel_wide, 8, axis=0), jnp.repeat(kernel_tall, 8, axis=0)
    act_flat = activations.transpose(1, 0, 2).reshape(pixels, chans)
    mixed, wide, tall = pl.pallas_call(
        functools.partial(front_kernel, n_row, n_col, rows, cols),
        out_shape=(jax.ShapeDtypeStruct((pixels, chans), f32), wide_shape, tall_shape),
        in_specs=[vmem] * 3,
        out_specs=(vmem,) * 3,
        scratch_shapes=halos + tile + [dma((4,)), dma((4,))],
        compiler_params=params(0),
    )(act_flat, kw, kt)
    grad_mixed, sum_in, sum_out = mlp_backward(
        mixed,
        cotangent.reshape(pixels, chans),
        norm_gain, norm_bias, weight_in, bias_in, weight_out, layer_scale,
    )
    factor = 1.0 / math.sqrt(pixels * n_row * n_col)
    hidden_units = weight_in.shape[1]
    big = jnp.concatenate(
        [sum_in[:, b : b + chans] for b in range(0, hidden_units, chans)] + [sum_out], axis=0
    ).astype(bf16)
    each = -(-2 * taps // (8 * n_row)) * 8
    small = jax.ShapeDtypeStruct((each * n_row, chans), f32)
    grad_flat, grad_in, grad_out, tapped = pl.pallas_call(
        functools.partial(back_kernel, n_row, n_col, rows, cols, factor),
        out_shape=(
            jax.ShapeDtypeStruct((pixels, chans), f32),
            jax.ShapeDtypeStruct(sum_in.shape, bf16),
            jax.ShapeDtypeStruct(sum_out.shape, bf16),
            small,
        ),
        in_specs=[vmem] * 6,
        out_specs=(vmem,) * 4,
        scratch_shapes=[pltpu.VMEM(tall_shape.shape, f32), pltpu.VMEM(wide_shape.shape, f32)]
        + halos[2:] + halos[:2] + tile
        + [pltpu.VMEM((8 * taps, chans), f32), pltpu.VMEM(small.shape, f32), dma((4,)), dma((4,))]
        + net_scratch(big, n_row, n_col)
        + net_scratch(small, n_row, n_col),
        compiler_params=params(1),
    )(grad_mixed, tall, wide, kw, kt, big)
    spread = grad_flat.reshape(cols, rows, chans).transpose(1, 0, 2)
    grad_input = (cotangent.astype(f32) + spread).astype(bf16)
    return (grad_input, grad_in, grad_out, tapped[:taps], tapped[taps : 2 * taps])


def solution(mesh):
    in_specs = (
        P("row", "col", None),
        P("row", "col", None),
        P(),
        P(),
        P(),
        P(),
        P(),
        P(),
        P(),
        P(),
    )
    out_specs = (P("row", "col", None), P(), P(), P(), P())
    return jax.shard_map(local, mesh=mesh, in_specs=in_specs, out_specs=out_specs, check_vma=False)
```

```python
import functools
import math

import jax
import jax.numpy as jnp
from jax import lax
from jax.experimental import pallas as pl
from jax.experimental.pallas import tpu as pltpu
from jax.sharding import PartitionSpec as P


def gelu_tanh(value):
    return jax.nn.gelu(value, approximate=True)


def mlp_backward(mixed, cot, norm_gain, norm_bias, weight_in, bias_in, weight_out, layer_scale):
    average = jnp.mean(mixed, axis=-1, keepdims=True)
    centred = mixed - average
    spread = jnp.mean(centred * centred, axis=-1, keepdims=True)
    rstd_val = lax.rsqrt(spread + 1e-06)
    unit = centred * rstd_val
    normed = (unit * norm_gain + norm_bias).astype(jnp.bfloat16)
    pre = jnp.dot(normed, weight_in, preferred_element_type=jnp.float32) + bias_in
    lifted_f, pullback = jax.vjp(gelu_tanh, pre)
    lifted = lifted_f.astype(jnp.bfloat16)
    scaled_cot = (layer_scale * cot.astype(jnp.float32)).astype(jnp.bfloat16)
    sum_out = jnp.dot(lifted.T, scaled_cot, preferred_element_type=jnp.float32)
    grad_lift = jnp.dot(scaled_cot, weight_out.T, preferred_element_type=jnp.float32)
    grad_pre = pullback(grad_lift)[0].astype(jnp.bfloat16)
    sum_in = jnp.dot(normed.T, grad_pre, preferred_element_type=jnp.float32)
    grad_unit = jnp.dot(grad_pre, weight_in.T, preferred_element_type=jnp.float32) * norm_gain
    first = jnp.mean(grad_unit, axis=-1, keepdims=True)
    second = jnp.mean(grad_unit * unit, axis=-1, keepdims=True)
    grad_mixed = (rstd_val * (grad_unit - first - unit * second)).astype(jnp.bfloat16)
    return (grad_mixed, sum_in, sum_out)


MESH = pl.DeviceIdType.MESH
GROUP = 8
LANES = 128


def remote(src, dst, send, recv, target):
    return pltpu.make_async_remote_copy(
        src_ref=src, dst_ref=dst, send_sem=send, recv_sem=recv, device_id=target, device_id_type=MESH
    )


def below(at, count):
    return (at + count - 1) // count


def above(at, count):
    return (2 * count - 2 - at) // count


def greet(barrier, target):
    pl.semaphore_signal(barrier, inc=1, device_id=target, device_id_type=MESH)


def taps_loop(acc, lo, hi, one, unroll=5):
    steps = max(hi - lo, 0) // unroll

    def body(s, acc):
        for u in range(unroll):
            acc = one(lo + s * unroll + u, acc)
        return acc

    if steps > 0:
        acc = lax.fori_loop(0, steps, body, acc)
    for o in range(lo + steps * unroll, hi):
        acc = one(o, acc)
    return acc


def conv_pass(padded, kernel, flip, minor, ranges, blocks, start, finish):
    last = kernel.shape[0] // 8 - 1
    size = GROUP * minor
    for b in blocks:

        @pl.loop(0, padded.shape[0])
        def _(part, b=b):
            lane = pl.ds(pl.multiple_of(part * LANES, LANES), LANES)

            def one(o, acc):
                tap_at = (last - o if flip else o) * 8
                tap_at = tap_at if isinstance(tap_at, int) else pl.multiple_of(tap_at, 8)
                tap = kernel[pl.ds(tap_at, 8), lane]
                at = b * size + o * minor
                at = at if isinstance(at, int) else pl.multiple_of(at, 8)
                return acc + tap[None] * padded[part, pl.ds(at, size), :].reshape(size // 8, 8, LANES)

            acc = start(b, lane).reshape(size // 8, 8, LANES)
            for lo, hi in ranges(b):
                acc = taps_loop(acc, lo, hi, one)
            finish(b, part, lane, acc.reshape(size, LANES))


def correlate(grad_at, grad, padded, taps, minor, sums, out, out_at):
    lead = (padded.shape[1] // minor) - taps + 1
    size = GROUP * minor
    for b in range(lead // GROUP):

        @pl.loop(0, padded.shape[0])
        def _(part, b=b):
            lane = pl.ds(pl.multiple_of(part * LANES, LANES), LANES)
            own = grad[part, pl.ds(grad_at + b * size, size), :]

            def one(o, carry):
                at = b * size + o * minor
                at = at if isinstance(at, int) else pl.multiple_of(at, 8)
                prod = own * padded[part, pl.ds(at, size), :]
                folded = jnp.sum(prod.reshape(size // 8, 8, LANES), axis=0)
                row = o * 8
                row = row if isinstance(row, int) else pl.multiple_of(row, 8)
                if b == 0:
                    sums[pl.ds(row, 8), lane] = folded
                else:
                    sums[pl.ds(row, 8), lane] = sums[pl.ds(row, 8), lane] + folded
                return carry

            taps_loop(0, 0, taps, one, 3)

    for t in range(taps):
        out[out_at + t : out_at + t + 1, :] = jnp.sum(sums[8 * t : 8 * t + 8, :], axis=0, keepdims=True)


def widen(src, padded, at):
    n = src.shape[0]
    for part in range(padded.shape[0]):
        lane = slice(part * LANES, (part + 1) * LANES)
        padded[part, at : at + n, :] = src[:, lane].astype(jnp.float32)


def narrow(padded, at, dst):
    n = dst.shape[0]
    for part in range(padded.shape[0]):
        lane = slice(part * LANES, (part + 1) * LANES)
        dst[:, lane] = padded[part, at : at + n, :].astype(dst.dtype)


class Halo:
    def __init__(self, at, count, target, src, low, high, sems):
        h = low.shape[0]
        top = src.shape[0] - h
        self.at, self.count, self.low, self.high = at, count, low, high
        self.up = remote(
            src.at[pl.ds(top, h)], low, sems.at[0], sems.at[1], target(lax.rem(at + 1, count))
        )
        self.down = remote(
            src.at[pl.ds(0, h)], high, sems.at[2], sems.at[3], target(lax.rem(at + count - 1, count))
        )

    def start(self):
        pl.when(self.at < self.count - 1)(self.up.start)
        pl.when(self.at > 0)(self.down.start)

    def clear(self, padded):
        h = self.low.shape[0]
        rest = padded.shape[1] - h
        zeros = jnp.zeros((padded.shape[0], h, LANES), jnp.float32)
        padded[:, 0:h, :] = zeros
        padded[:, rest : rest + h, :] = zeros

    def finish(self, padded):
        h = self.low.shape[0]
        rest = padded.shape[1] - h

        @pl.when(self.at > 0)
        def _():
            self.up.wait_recv()
            widen(self.low, padded, 0)
            self.down.wait_send()

        @pl.when(self.at < self.count - 1)
        def _():
            self.down.wait_recv()
            widen(self.high, padded, rest)
            self.up.wait_send()


def inner_range(lead, reach):
    return lambda b: [(max(reach - GROUP * b, 0), lead + reach - GROUP * b - GROUP + 1)]


def outer_range(lead, reach):
    def ranges(b):
        lo, hi = inner_range(lead, reach)(b)[0]
        return [(0, lo), (hi, 2 * reach + 1)]

    return ranges


def no_start(size):
    return lambda b, lane: jnp.zeros((size, LANES), jnp.float32)


def transposing(dst, at, inner, outer):
    def finish(b, part, lane, acc):
        value = acc.astype(jnp.bfloat16).astype(jnp.float32)
        for g in range(GROUP):
            dst[part, pl.ds(at + b * GROUP + g, inner, stride=outer), :] = value[g * inner : (g + 1) * inner]

    return finish


def into(dst, size):
    def finish(b, part, lane, acc):
        dst[pl.ds(b * size, size), lane] = acc

    return finish


def out_of(src, size):
    return lambda b, lane: src[pl.ds(b * size, size), lane]


def front_kernel(
    n_row, n_col, rows, cols, act, kw, kt, mixed, wide, tall, low_a, high_a, low_h, high_h, hid, part, sem_a, sem_h
):
    row, col = lax.axis_index("row"), lax.axis_index("col")
    barrier = pltpu.get_barrier_semaphore()
    reach = kw.shape[0] // 16
    for at, count, target in (
        (row, n_row, lambda i: (i, col)),
        (col, n_col, lambda i: (row, i)),
    ):
        pl.when(at > 0)(lambda at=at, target=target: greet(barrier, target(at - 1)))
        pl.when(at < count - 1)(lambda at=at, target=target: greet(barrier, target(at + 1)))
    greeted = below(row, n_row) + above(row, n_row) + below(col, n_col) + above(col, n_col)
    pl.semaphore_wait(barrier, greeted)
    halo = Halo(col, n_col, lambda i: (row, i), act, low_a, high_a, sem_a)
    halo.start()
    halo.clear(wide)
    widen(act, wide, reach * rows)
    blocks, size = range(cols // GROUP), GROUP * rows
    conv_pass(wide, kw, False, rows, inner_range(cols, reach), blocks, no_start(size), into(part, size))
    halo.finish(wide)
    conv_pass(
        wide, kw, False, rows, outer_range(cols, reach), blocks, out_of(part, size),
        transposing(tall, reach * cols, rows, cols),
    )
    narrow(tall, reach * cols, hid)
    halo = Halo(row, n_row, lambda i: (i, col), hid, low_h, high_h, sem_h)
    halo.start()
    halo.clear(tall)
    blocks, size = range(rows // GROUP), GROUP * cols
    conv_pass(tall, kt, False, cols, inner_range(rows, reach), blocks, no_start(size), into(part, size))
    halo.finish(tall)
    conv_pass(
        tall, kt, False, cols, outer_range(rows, reach), blocks, out_of(part, size), into(mixed, size)
    )


class Net:
    def __init__(self, n_row, n_col, factor, src, scratch):
        self.src, self.n_col, self.factor = src, n_col, factor
        self.pair_buf, self.half, self.slots, self.cols, self.whole = scratch[:5]
        self.sems = scratch[5:]
        self.row, self.col = lax.axis_index("row"), lax.axis_index("col")
        self.m = n_row // 2
        self.core, self.j = lax.rem(self.row, 2), self.row // 2
        self.pair = (self.row + 1 - 2 * self.core, self.col)
        self.p = self.slots.shape[1]
        self.h = self.half.shape[0]

    def peer(self, d):
        return (2 * lax.rem(self.j + d, self.m) + self.core, self.col)

    def col_peer(self, d):
        return (self.row, lax.rem(self.col + d, self.n_col))

    def pair_copy(self):
        other = pl.multiple_of((1 - self.core) * self.h, 16)
        return remote(self.src.at[pl.ds(other, self.h)], self.pair_buf, self.sems[0], self.sems[1], self.pair)

    def peer_copy(self, d):
        at = pl.multiple_of(lax.rem(self.j + d, self.m) * self.p, self.p)
        return remote(
            self.half.at[pl.ds(at, self.p)], self.slots.at[d], self.sems[2].at[d], self.sems[3].at[d], self.peer(d)
        )

    def col_copy(self, d, c):
        return remote(self.cols.at[c], self.cols.at[c], self.sems[4].at[d], self.sems[5].at[c], self.col_peer(d))

    def back_copy(self, d, owner):
        at = pl.multiple_of(self.core * self.h + owner * self.p, self.p)
        part = self.whole.at[pl.ds(at, self.p)]
        return remote(part, part, self.sems[6].at[d], self.sems[7].at[d], self.peer(d))

    def last_copy(self, side):
        part = self.whole.at[pl.ds(pl.multiple_of(side * self.h, 16), self.h)]
        return remote(part, part, self.sems[8], self.sems[9], self.pair)

    def step_pair(self):
        self.pair_copy().start()

    def step_peers(self):
        self.pair_copy().wait()
        at = pl.multiple_of(self.core * self.h, 16)
        mine = self.src[pl.ds(at, self.h), :].astype(jnp.float32)
        self.half[...] = (mine + self.pair_buf[...].astype(jnp.float32)).astype(self.half.dtype)

        @pl.loop(1, self.m)
        def _(d):
            self.peer_copy(d).start()

    def step_cols(self):
        at = pl.multiple_of(self.j * self.p, self.p)
        self.cols[self.col] = self.half[pl.ds(at, self.p), :].astype(jnp.float32)

        @pl.loop(1, self.m)
        def _(d):
            self.peer_copy(d).wait()
            self.cols[self.col] = self.cols[self.col] + self.slots[d].astype(jnp.float32)

        @pl.loop(1, self.n_col)
        def _(d):
            self.col_copy(d, self.col).start()

    def step_back(self):
        @pl.loop(1, self.n_col)
        def _(d):
            self.col_copy(d, self.col).wait_send()
            self.col_copy(d, lax.rem(self.col + d, self.n_col)).wait_recv()

        total = self.cols[0]
        for c in range(1, self.n_col):
            total = total + self.cols[c]
        at = pl.multiple_of(self.core * self.h + self.j * self.p, self.p)
        self.whole[pl.ds(at, self.p), :] = (total * self.factor).astype(self.whole.dtype)

        @pl.loop(1, self.m)
        def _(d):
            self.back_copy(d, self.j).start()

    def step_last(self):
        @pl.loop(1, self.m)
        def _(d):
            self.back_copy(d, self.j).wait_send()
            self.back_copy(d, lax.rem(self.j + self.m - d, self.m)).wait_recv()

        self.last_copy(self.core).start()

    def step_end(self):
        self.last_copy(self.core).wait_send()
        self.last_copy(1 - self.core).wait_recv()


def back_kernel(
    n_row, n_col, rows, cols, factor, gm, tall, wide, kw, kt, big, gin, in_out, out_out, small_out,
    gpad, hpad, low_g, high_g, low_h, high_h, ghb, part, sums, small, sem_g, sem_h, *scratch
):
    row, col = lax.axis_index("row"), lax.axis_index("col")
    reach, taps = kw.shape[0] // 16, kw.shape[0] // 8
    net = Net(n_row, n_col, factor, big, scratch[:15])
    net2 = Net(n_row, n_col, factor, small, scratch[15:])
    barrier = pltpu.get_barrier_semaphore()
    other = row - 1 + 2 * net.core
    present = jnp.logical_and(other >= 0, other < n_row)
    greet(barrier, net.pair)
    pl.when(present)(lambda: greet(barrier, (other, col)))

    @pl.loop(1, net.m)
    def _(d):
        greet(barrier, net.peer(d))

    @pl.loop(1, n_col)
    def _(d):
        greet(barrier, net.col_peer(d))

    more = (1 - net.core) * below(row, n_row) + net.core * above(row, n_row)
    pl.semaphore_wait(barrier, 1 + (net.m - 1) + (n_col - 1) + more)

    halo = Halo(row, n_row, lambda i: (i, col), gm, low_g, high_g, sem_g)
    halo.start()
    net.step_pair()
    halo.clear(gpad)
    widen(gm, gpad, reach * cols)
    small[2 * taps :, :] = jnp.zeros((small.shape[0] - 2 * taps, small.shape[1]), jnp.float32)
    net.step_peers()
    correlate(reach * cols, gpad, tall, taps, cols, sums, small, taps)
    halo.finish(gpad)
    blocks, size = range(rows // GROUP), GROUP * cols
    conv_pass(
        gpad, kt, True, cols, lambda b: [(0, taps)], blocks, no_start(size),
        transposing(hpad, reach * rows, cols, rows),
    )
    net.step_cols()
    narrow(hpad, reach * rows, ghb)
    halo = Halo(col, n_col, lambda i: (row, i), ghb, low_h, high_h, sem_h)
    halo.start()
    halo.clear(hpad)
    correlate(reach * rows, hpad, wide, taps, rows, sums, small, 0)
    net2.step_pair()
    net.step_back()
    blocks, size = range(cols // GROUP), GROUP * rows
    conv_pass(hpad, kw, True, rows, inner_range(cols, reach), blocks, no_start(size), into(part, size))
    net2.step_peers()
    halo.finish(hpad)
    half = len(blocks) // 2
    outer = outer_range(cols, reach)
    conv_pass(hpad, kw, True, rows, outer, blocks[:half], out_of(part, size), into(gin, size))
    net2.step_cols()
    conv_pass(hpad, kw, True, rows, outer, blocks[half:], out_of(part, size), into(gin, size))
    net2.step_back()
    net.step_last()
    net2.step_last()
    net.step_end()
    net2.step_end()
    depth, width = in_out.shape[0], net.whole.shape[1]
    inner = in_out.shape[1] // width
    for b in range(inner):
        in_out[:, b * width : (b + 1) * width] = net.whole[b * depth : (b + 1) * depth, :]
    out_out[...] = net.whole[inner * depth :, :]
    small_out[...] = net2.whole[...]


def net_scratch(src, n_row, n_col):
    rows, width = src.shape
    p, m = rows // n_row, n_row // 2
    dma = pltpu.SemaphoreType.DMA
    return [
        pltpu.VMEM((rows // 2, width), src.dtype),
        pltpu.VMEM((rows // 2, width), src.dtype),
        pltpu.VMEM((m, p, width), src.dtype),
        pltpu.VMEM((n_col, p, width), jnp.float32),
        pltpu.VMEM((rows, width), src.dtype),
        dma, dma, dma((m,)), dma((m,)), dma((n_col,)), dma((n_col,)), dma((m,)), dma((m,)), dma, dma,
    ]


def params(number):
    return pltpu.CompilerParams(
        collective_id=number, has_side_effects=True, vmem_limit_bytes=40 * 1024 * 1024
    )


def local(
    activations, cotangent, kernel_wide, kernel_tall, norm_gain, norm_bias, weight_in, bias_in, weight_out, layer_scale
):
    rows, cols, chans = activations.shape
    taps = kernel_wide.shape[0]
    reach = taps // 2
    n_row, n_col = lax.axis_size("row"), lax.axis_size("col")
    pixels = rows * cols
    f32, bf16 = jnp.float32, jnp.bfloat16
    vmem = pl.BlockSpec(memory_space=pltpu.VMEM)
    dma = pltpu.SemaphoreType.DMA
    wide_shape = jax.ShapeDtypeStruct((chans // LANES, (cols + 2 * reach) * rows, LANES), f32)
    tall_shape = jax.ShapeDtypeStruct((chans // LANES, (rows + 2 * reach) * cols, LANES), f32)
    halos = [
        pltpu.VMEM((reach * rows, chans), bf16),
        pltpu.VMEM((reach * rows, chans), bf16),
        pltpu.VMEM((reach * cols, chans), bf16),
        pltpu.VMEM((reach * cols, chans), bf16),
    ]
    tile = [pltpu.VMEM((pixels, chans), bf16), pltpu.VMEM((pixels, chans), f32)]
    kw, kt = jnp.repeat(kernel_wide, 8, axis=0), jnp.repeat(kernel_tall, 8, axis=0)
    act_flat = activations.transpose(1, 0, 2).reshape(pixels, chans)
    mixed, wide, tall = pl.pallas_call(
        functools.partial(front_kernel, n_row, n_col, rows, cols),
        out_shape=(jax.ShapeDtypeStruct((pixels, chans), f32), wide_shape, tall_shape),
        in_specs=[vmem] * 3,
        out_specs=(vmem,) * 3,
        scratch_shapes=halos + tile + [dma((4,)), dma((4,))],
        compiler_params=params(0),
    )(act_flat, kw, kt)
    grad_mixed, sum_in, sum_out = mlp_backward(
        mixed,
        cotangent.reshape(pixels, chans),
        norm_gain, norm_bias, weight_in, bias_in, weight_out, layer_scale,
    )
    factor = 1.0 / math.sqrt(pixels * n_row * n_col)
    hidden_units = weight_in.shape[1]
    big = jnp.concatenate(
        [sum_in[:, b : b + chans] for b in range(0, hidden_units, chans)] + [sum_out], axis=0
    ).astype(bf16)
    each = -(-2 * taps // (8 * n_row)) * 8
    small = jax.ShapeDtypeStruct((each * n_row, chans), f32)
    grad_flat, grad_in, grad_out, tapped = pl.pallas_call(
        functools.partial(back_kernel, n_row, n_col, rows, cols, factor),
        out_shape=(
            jax.ShapeDtypeStruct((pixels, chans), f32),
            jax.ShapeDtypeStruct(sum_in.shape, bf16),
            jax.ShapeDtypeStruct(sum_out.shape, bf16),
            small,
        ),
        in_specs=[vmem] * 6,
        out_specs=(vmem,) * 4,
        scratch_shapes=[pltpu.VMEM(tall_shape.shape, f32), pltpu.VMEM(wide_shape.shape, f32)]
        + halos[2:] + halos[:2] + tile
        + [pltpu.VMEM((8 * taps, chans), f32), pltpu.VMEM(small.shape, f32), dma((4,)), dma((4,))]
        + net_scratch(big, n_row, n_col)
        + net_scratch(small, n_row, n_col),
        compiler_params=params(1),
    )(grad_mixed, tall, wide, kw, kt, big)
    spread = grad_flat.reshape(cols, rows, chans).transpose(1, 0, 2)
    grad_input = (cotangent.astype(f32) + spread).astype(bf16)
    return (grad_input, grad_in, grad_out, tapped[:taps], tapped[taps : 2 * taps])


def solution(mesh):
    in_specs = (
        P("row", "col", None),
        P("row", "col", None),
        P(),
        P(),
        P(),
        P(),
        P(),
        P(),
        P(),
        P(),
    )
    out_specs = (P("row", "col", None), P(), P(), P(), P())
    return jax.shard_map(local, mesh=mesh, in_specs=in_specs, out_specs=out_specs, check_vma=False)
```
